512 devices in a mesh: depth: 8 (over z), tile: 64 (over y, x, core).
Axes of the slice: x: 4, y: 8, z: 8, core: 2. Of those that a mesh axis runs over, the one named last changes fastest.
Arguments:
- exit_grad: bfloat16 [256, 256, 2, 256], P('tile', 'depth'), may hold values from -6 to 6
- stored_waves: bfloat16 [16, 256, 256, 2, 256], P('depth', 'tile'), may hold values from -6 to 6
- object_slices: float32 [16, 448, 2, 16384], P('depth', None, None, 'tile'), may hold values from -4 to 4
- propagator_taps: float32 [2, 2, 31], replicated, may hold values from -0.75 to 0.75
- positions: int32 [256, 2], replicated, may hold values from 0 to 255, as said below
- counts: int32 [64], replicated, may hold values from 1 to 4, as said below
Outputs:
- object_grad: bfloat16 [16, 448, 2, 16384], P('depth', None, None, 'tile')
The draws below stay inside these ranges and needn't reach their ends.
Inputs may be any that keep to these rules, and one draw needn't show every extreme that they name: Column 0 is a window's first row, 0 to 192; column 1 is a window's centre column within its tile, 0 to 255. Dead slots hold positions too. `counts`: some tile has exactly 4 live slots and some tile exactly 1.
All inputs are finite; a program needn't handle non-finite values.
Results may differ from the reference program's by a relative error of at most 0.034.
Values may be sent and summed in bfloat16 or wider, within the bound.
A program may use at most 64 MiB of HBM per device.

```python
import jax
import jax.numpy as jnp
from jax import lax

PROBE = 256
TAPS = 31
CAP = 4
TILE_COLS = 256
ROWS = 448
TILES = 64
SLOTS = 256
SLICES = 16
OBJ_COLS = 16384


def draw_counts(key, part):
    subkeys = jax.random.split(jax.random.fold_in(key, 11), 3)
    draw_level = jax.random.randint(subkeys[0], (TILES,), 0, 100)
    level_cubed = draw_level * draw_level * draw_level
    counts_drawn = 1 + (CAP - 1) * level_cubed // 970299
    busiest = jax.random.randint(subkeys[1], (), 0, TILES)
    lightest = (busiest + 1 + jax.random.randint(subkeys[2], (), 0, TILES - 1)) % TILES
    counts_drawn = counts_drawn.at[busiest].set(CAP)
    counts_drawn = counts_drawn.at[lightest].set(1)
    return counts_drawn.astype(jnp.int32)


def draw_positions(key, part):
    subkeys = jax.random.split(jax.random.fold_in(key, 23), 2)
    row_starts = jax.random.randint(subkeys[0], (SLOTS,), 0, ROWS - PROBE + 1)
    column_starts = jax.random.randint(subkeys[1], (SLOTS,), 0, TILE_COLS)
    last_first = (TILES - 1) * CAP
    row_starts = row_starts.at[0].set(0).at[last_first].set(ROWS - PROBE)
    column_starts = column_starts.at[0].set(0).at[last_first].set(TILE_COLS - 1)
    return jnp.stack([row_starts, column_starts], axis=1).astype(jnp.int32)


def levels(rng, shape, shards, smallest, top_value):
    factor_of = 1.0
    for dim, parts in shards:
        draws = jax.random.uniform(jax.random.fold_in(jax.random.fold_in(rng, 6), dim), (parts,), jnp.float32, smallest / len(shards), top_value / len(shards))
        factor_of = factor_of * jnp.repeat(jnp.exp(draws), shape[dim] // parts).reshape((-1,) + (1,) * (len(shape) - 1 - dim))
    return factor_of


def gaussian(own_key, shape, spread, limit, cuts=(), kind=jnp.bfloat16):
    drawn = jax.random.normal(own_key, shape, jnp.float32) * spread
    if len(cuts) > 0:
        drawn = levels(own_key, shape, cuts, -0.22, 0.18) * drawn
    return jnp.clip(drawn, min=-limit, max=limit).astype(kind)


def setup_inputs(seed: int = 0) -> dict:
    splits = jax.random.split(jax.random.key(seed), 7)
    return {
        "exit_grad": gaussian(splits[0], (SLOTS, PROBE, 2, PROBE), 1.0, 6.0, ((0, 64), (1, 8))),
        "stored_waves": gaussian(splits[1], (SLICES, SLOTS, PROBE, 2, PROBE), 1.0, 6.0, ((0, 8), (1, 64))),
        "object_slices": gaussian(splits[2], (SLICES, ROWS, 2, OBJ_COLS), 0.7, 4.0, ((0, 8), (3, 64)), jnp.float32),
        "propagator_taps": gaussian(splits[3], (2, 2, TAPS), (2 * TAPS) ** -0.5, 0.75, (), jnp.float32),
        "positions": draw_positions(jax.random.fold_in(splits[6], 71), 0),
        "counts": draw_counts(jax.random.fold_in(splits[6], 71), 0),
    }


def band_blocks(propagator_taps, probe_side):
    tap_count = propagator_taps.shape[2]
    centre = tap_count // 2
    places = jnp.arange(probe_side, dtype=jnp.int32)
    offset = places[None, :] - places[:, None] + centre
    onehot = (offset.reshape(1, probe_side * probe_side) == jnp.arange(tap_count, dtype=jnp.int32)[:, None]).astype(jnp.float32)
    flat_taps = jnp.dot(propagator_taps.reshape(4, tap_count), onehot, precision=lax.Precision.HIGHEST, preferred_element_type=jnp.float32)
    matrices = flat_taps.reshape(2, 2, probe_side, probe_side)
    y_real, y_imag = matrices[0, 0], matrices[0, 1]
    x_real, x_imag = matrices[1, 0], matrices[1, 1]
    column_block = jnp.concatenate([jnp.concatenate([x_real, -x_imag], 1), jnp.concatenate([x_imag, x_real], 1)], 0).astype(jnp.bfloat16)
    row_block = jnp.concatenate([y_real.T, y_imag.T], 0).astype(jnp.bfloat16)
    return column_block, row_block


def propagate(wave_block, column_block, row_block):
    probe_side = wave_block.shape[1]
    flat_waves = wave_block.reshape(wave_block.shape[0], probe_side, 2 * probe_side).astype(jnp.float32)
    mixed = jnp.einsum("mrc,cd->mrd", flat_waves, column_block.astype(jnp.float32), precision=lax.Precision.HIGHEST).astype(jnp.bfloat16)
    stacked = jnp.einsum("ar,mrd->mad", row_block.astype(jnp.float32), mixed.astype(jnp.float32), precision=lax.Precision.HIGHEST)
    upper_half = stacked[:, :probe_side]
    lower_half = stacked[:, probe_side:]
    wave_real = upper_half[:, :, :probe_side] + lower_half[:, :, probe_side:]
    wave_imag = upper_half[:, :, probe_side:] - lower_half[:, :, :probe_side]
    return wave_real, wave_imag


def reference(exit_grad, stored_waves, object_slices, propagator_taps, positions, counts):
    probe_side = exit_grad.shape[1]
    half_side = probe_side // 2
    column_block, row_block = band_blocks(propagator_taps, probe_side)
    slot_ids = jnp.arange(positions.shape[0], dtype=jnp.int32)
    slot_owner = slot_ids // CAP
    live_weight = (slot_ids % CAP < counts[slot_owner]).astype(jnp.float32)
    row_starts = positions[:, 0].astype(jnp.int32)
    column_starts = (slot_owner * TILE_COLS + positions[:, 1]).astype(jnp.int32)
    row_count = object_slices.shape[1]
    wave_now = exit_grad
    slice_grads = []
    for slice_index in range(SLICES - 1, -1, -1):
        slab = object_slices[slice_index]
        extended = jnp.concatenate([slab[:, :, OBJ_COLS - half_side:], slab, slab[:, :, :half_side]], axis=2)

        def per_slot(accumulator, slot_item):
            wave_one, stored, row_start, col_start, weight = slot_item
            wave_real, wave_imag = propagate(wave_one[None], column_block, row_block)
            wave_real = wave_real[0]
            wave_imag = wave_imag[0]
            zero_index = jnp.zeros((), jnp.int32)
            window = lax.dynamic_slice(extended, (row_start, zero_index, col_start), (probe_side, 2, probe_side))
            stored_real = stored[:, 0].astype(jnp.float32)
            stored_imag = stored[:, 1].astype(jnp.float32)
            grad_real = stored_real * wave_real + stored_imag * wave_imag
            grad_imag = stored_real * wave_imag - stored_imag * wave_real
            term = jnp.stack([grad_real, grad_imag], 1) * weight
            region = lax.dynamic_slice(accumulator, (row_start, zero_index, col_start), (probe_side, 2, probe_side))
            accumulator = lax.dynamic_update_slice(accumulator, region + term, (row_start, zero_index, col_start))
            obj_real = window[:, 0]
            obj_imag = window[:, 1]
            out_wave = jnp.stack([obj_real * wave_real + obj_imag * wave_imag, obj_real * wave_imag - obj_imag * wave_real], 1).astype(jnp.bfloat16)
            return accumulator, out_wave

        start_acc = jnp.zeros((row_count, 2, OBJ_COLS + probe_side), jnp.float32)
        accumulator, wave_now = lax.scan(per_slot, start_acc, (wave_now, stored_waves[slice_index], row_starts, column_starts, live_weight))
        owned_part = accumulator[:, :, half_side:half_side + OBJ_COLS]
        owned_part = owned_part.at[:, :, :half_side].add(accumulator[:, :, OBJ_COLS + half_side:])
        owned_part = owned_part.at[:, :, OBJ_COLS - half_side:].add(accumulator[:, :, :half_side])
        slice_grads.append(owned_part.astype(jnp.bfloat16))
    return jnp.stack(slice_grads[::-1])
```

```python
import functools

import jax
import jax.numpy as jnp
from jax import lax
from jax.experimental import pallas as pl
from jax.experimental.pallas import tpu as pltpu
from jax.sharding import PartitionSpec as P

MESH = pl.DeviceIdType.MESH
F32 = jnp.float32
BF16 = jnp.bfloat16

NEED = (96, 160, 224, 256)
FIRST = (80, 144, 208, 256)
SECOND = (64, 128, 192, 256)
PIECE = 32
PAD = 16
BAND = 128
TALL = 80
ROW_STEP = 64


def kernel(
    groups,
    tiles,
    pos_ref,
    cnt_ref,
    taps_ref,
    exit_ref,
    obj_ref,
    st_hbm,
    out_ref,
    waves,
    sends,
    exits,
    ext,
    win,
    back,
    acc,
    place,
    flat,
    inter,
    stored,
    mixer,
    tall,
    mixed,
    rim_send,
    rim_recv,
    grad_send,
    grad_recv,
    recv_sem,
    send_sem,
    exit_sem,
    rim_send_sem,
    rim_recv_sem,
    grad_send_sem,
    grad_recv_sem,
    st_sem,
):
    g = lax.axis_index("depth")
    t = lax.axis_index("tile")
    last = groups - 1
    side = mixer.shape[0] // 2
    slots = waves.shape[0]
    rows = ext.shape[3]
    right = lax.rem(t + 1, tiles)
    left = lax.rem(t + tiles - 1, tiles)

    barrier = pltpu.get_barrier_semaphore()

    def greet(group, tile):
        pl.semaphore_signal(barrier, inc=1, device_id=(group, tile), device_id_type=MESH)

    greet(g, right)
    greet(g, left)

    @pl.when(g == last)
    def _():
        for other in range(last):
            greet(other, t)

    @pl.when(g < last)
    def _():
        greet(last, t)

    @pl.when(g < last - 1)
    def _():
        greet(g + 1, t)

    @pl.when((g > 0) & (g < last))
    def _():
        greet(g - 1, t)

    st_copy = pltpu.make_async_copy(st_hbm, stored, st_sem)
    st_copy.start()

    own_rows = exits.shape[1]
    flat[: slots * own_rows * 4, :] = exit_ref[...].astype(F32)
    for s in range(slots):
        for part in range(2):
            for half in range(2):
                lane = part * side + half * 128
                exits[s, :, lane : lane + 128] = flat[
                    pl.ds(s * own_rows * 4 + half * 2 + part, own_rows, stride=4), :
                ].astype(BF16)

    def spread(layer):
        for part in range(2):
            for half in range(2):
                plane = obj_ref[pl.ds(layer * rows * 4 + half * 2 + part, rows, stride=4), :]
                ext[layer, part, 1 + half] = plane
                rim_send[half, layer, part] = plane.astype(BF16)

    spread(1)

    @pl.when((g == 0) | (g == last - 1))
    def _():
        pl.semaphore_wait(barrier, 4)

    @pl.when((g > 0) & (g < last - 1))
    def _():
        pl.semaphore_wait(barrier, 5)

    @pl.when(g == last)
    def _():
        pl.semaphore_wait(barrier, last + 2)

    def exit_copy(s):
        return pltpu.make_async_remote_copy(
            src_ref=exits.at[s],
            dst_ref=waves.at[s, pl.ds(pl.multiple_of(g * PIECE, PIECE), PIECE), :],
            send_sem=exit_sem.at[s],
            recv_sem=recv_sem.at[s, g],
            device_id=(last, t),
            device_id_type=MESH,
        )

    def own_exit(s):
        return pltpu.make_async_copy(
            exits.at[s],
            waves.at[s, pl.ds(last * PIECE, PIECE), :],
            recv_sem.at[s, last],
        )

    @pl.when(g < last)
    def _():
        for s in range(slots):
            exit_copy(s).start()

    @pl.when(g == last)
    def _():
        for s in range(slots):
            own_exit(s).start()

    def rim_copy(half, layer):
        return pltpu.make_async_remote_copy(
            src_ref=rim_send.at[half, layer],
            dst_ref=rim_recv.at[half, layer],
            send_sem=rim_send_sem.at[half, layer],
            recv_sem=rim_recv_sem.at[half, layer],
            device_id=(g, left if half == 0 else right),
            device_id_type=MESH,
        )

    def grad_copy(half, layer):
        return pltpu.make_async_remote_copy(
            src_ref=grad_send.at[half, layer],
            dst_ref=grad_recv.at[half, layer],
            send_sem=grad_send_sem.at[half, layer],
            recv_sem=grad_recv_sem.at[half, layer],
            device_id=(g, left if half == 0 else right),
            device_id_type=MESH,
        )

    rim_copy(0, 1).start()
    rim_copy(1, 1).start()
    spread(0)
    rim_copy(0, 0).start()
    rim_copy(1, 0).start()

    def mixer_rows(i, carry):
        start = pl.multiple_of(i * 32, 32)
        row = lax.broadcasted_iota(jnp.int32, (32, side), 0) + start
        column = lax.broadcasted_iota(jnp.int32, (32, side), 1)
        tap = column - row + 15
        real = jnp.zeros((32, side), F32)
        imag = jnp.zeros((32, side), F32)
        for k in range(31):
            hit = tap == k
            real = jnp.where(hit, taps_ref[2, k], real)
            imag = jnp.where(hit, taps_ref[3, k], imag)
        real = real.astype(BF16)
        imag = imag.astype(BF16)
        mixer[pl.ds(start, 32), :side] = real
        mixer[pl.ds(start, 32), side:] = -imag
        mixer[pl.ds(side + start, 32), :side] = imag
        mixer[pl.ds(side + start, 32), side:] = real
        return carry

    lax.fori_loop(0, side // 32, mixer_rows, 0)

    row = lax.broadcasted_iota(jnp.int32, (TALL, BAND), 0)
    column = lax.broadcasted_iota(jnp.int32, (TALL, BAND), 1)
    tap = row - column + 15 + PAD
    real = jnp.zeros((TALL, BAND), F32)
    imag = jnp.zeros((TALL, BAND), F32)
    for k in range(31):
        hit = tap == k
        real = jnp.where(hit, taps_ref[0, k], real)
        imag = jnp.where(hit, taps_ref[1, k], imag)
    tall[0, :, :BAND] = real.astype(BF16)
    tall[0, :, BAND:] = imag.astype(BF16)
    tall[1, :, :BAND] = -imag.astype(BF16)
    tall[1, :, BAND:] = real.astype(BF16)

    mixed[...] = jnp.zeros(mixed.shape, BF16)

    first_slot = t * slots

    def windows(s, layer):
        row_start = pos_ref[0, first_slot + s]
        shift = lax.rem(512 - pos_ref[1, first_slot + s], 512)

        def some(i, carry):
            begin = pl.multiple_of(i * ROW_STEP, ROW_STEP)
            for part in range(2):
                blocks = [ext[layer, part, c, pl.ds(row_start + begin, ROW_STEP), :] for c in range(4)]
                turned = pltpu.roll(jnp.concatenate(blocks, axis=1), shift, 1)
                win[layer, s, part, pl.ds(begin, ROW_STEP), :] = turned[:, :side]
            return carry

        lax.fori_loop(0, side // ROW_STEP, some, 0)

    def rim_arrived(layer):
        rim_copy(0, layer).wait_recv()
        rim_copy(1, layer).wait_recv()
        ext[layer, :, 3] = rim_recv[0, layer].astype(F32)
        ext[layer, :, 0] = rim_recv[1, layer].astype(F32)

    rim_arrived(1)
    windows(0, 1)
    rim_arrived(0)
    windows(0, 0)

    @pl.when(g < last)
    def _():
        def some(s, carry):
            windows(s, 1)
            windows(s, 0)
            return carry

        lax.fori_loop(1, slots, some, 0)

    place[...] = jnp.zeros(place.shape, F32)
    acc[...] = jnp.zeros(acc.shape, F32)
    st_copy.wait()

    def piece_copy(s, j):
        span = pl.ds(j * PIECE, PIECE)
        return pltpu.make_async_remote_copy(
            src_ref=sends.at[s, span, :],
            dst_ref=waves.at[s, span, :],
            send_sem=send_sem.at[s, j],
            recv_sem=recv_sem.at[s, j],
            device_id=(g - 1, t),
            device_id_type=MESH,
        )

    def mix(layer, wave, begin):
        v = jnp.dot(wave, mixer[...], preferred_element_type=F32).astype(BF16)
        n = wave.shape[0]
        mixed[layer, 0, PAD + begin : PAD + begin + n, :] = v[:, :side]
        mixed[layer, 1, PAD + begin : PAD + begin + n, :] = v[:, side:]

    def leave(s, layer, begin, end):
        n = end - begin
        lhs = jnp.concatenate([tall[0, :n, :], tall[1, :n, :]], axis=0)
        rhs = jnp.concatenate(
            [mixed[layer, 0, begin : begin + BAND, :], mixed[layer, 1, begin : begin + BAND, :]], axis=0
        )
        h = jnp.dot(lhs, rhs, preferred_element_type=F32)
        real = h[:n]
        imag = h[n:]
        back[layer, 0, begin:end, :] = real
        back[layer, 1, begin:end, :] = imag
        obj_real = win[layer, s, 0, begin:end, :]
        obj_imag = win[layer, s, 1, begin:end, :]
        return jnp.concatenate(
            [obj_real * real + obj_imag * imag, obj_real * imag - obj_imag * real], axis=1
        ).astype(BF16)

    def relay(s):
        came = first_end = second_end = 0
        for step in range(4):
            for j in range(came // PIECE, NEED[step] // PIECE):
                piece_copy(s, j).wait_recv()
            mix(1, waves[s, came : NEED[step], :], came)
            wave = leave(s, 1, first_end, FIRST[step])
            mix(0, wave, first_end)
            sends[s, second_end : SECOND[step], :] = leave(s, 0, second_end, SECOND[step])

            @pl.when(g > 0)
            def _():
                for j in range(second_end // PIECE, SECOND[step] // PIECE):
                    piece_copy(s, j).start()

            came, first_end, second_end = NEED[step], FIRST[step], SECOND[step]

    def gather_grad(s, layer):
        row_start = pos_ref[0, first_slot + s]
        shift = pos_ref[1, first_slot + s]
        live = s < cnt_ref[t]
        begin = pl.multiple_of((layer * slots + s) * side * 4, side * 4)
        flat[...] = stored[pl.ds(begin, side * 4), :].astype(F32)

        def some(i, carry):
            at = pl.multiple_of(i * ROW_STEP, ROW_STEP)
            planes = [flat[pl.ds(at * 4 + q, ROW_STEP, stride=4), :] for q in range(4)]
            st_real = jnp.concatenate([planes[0], planes[2]], axis=1)
            st_imag = jnp.concatenate([planes[1], planes[3]], axis=1)
            real = back[layer, 0, pl.ds(at, ROW_STEP), :]
            imag = back[layer, 1, pl.ds(at, ROW_STEP), :]
            terms = (st_real * real + st_imag * imag, st_real * imag - st_imag * real)
            for part in range(2):
                term = jnp.where(live, terms[part], 0.0)
                wide = jnp.concatenate([term, jnp.zeros((ROW_STEP, side), F32)], axis=1)
                wide = pltpu.roll(wide, shift, 1)
                for c in range(4):
                    place[part, c, pl.ds(rows - side + at, ROW_STEP), :] = wide[:, c * 128 : c * 128 + 128]
            return carry

        lax.fori_loop(0, side // ROW_STEP, some, 0)

        def add(i, carry):
            at = pl.multiple_of(i * ROW_STEP, ROW_STEP)
            for part in range(2):
                for c in range(4):
                    acc[layer, part, c, pl.ds(at, ROW_STEP), :] += place[
                        part, c, pl.ds(rows - side - row_start + at, ROW_STEP), :
                    ]
            return carry

        lax.fori_loop(0, rows // ROW_STEP, add, 0)

    def send_grad(layer):
        grad_send[0, layer] = acc[layer, :, 0].astype(BF16)
        grad_send[1, layer] = acc[layer, :, 3].astype(BF16)
        grad_copy(0, layer).start()
        grad_copy(1, layer).start()

    def turn(s, carry):
        relay(s)

        @pl.when((g == last) & (s < slots - 1))
        def _():
            windows(s + 1, 1)
            windows(s + 1, 0)

        gather_grad(s, 1)

        @pl.when(s == slots - 1)
        def _():
            send_grad(1)

        gather_grad(s, 0)
        return carry

    lax.fori_loop(0, slots, turn, 0)
    send_grad(0)

    for layer in (1, 0):
        grad_copy(0, layer).wait_recv()
        grad_copy(1, layer).wait_recv()
        for part in range(2):
            first = acc[layer, part, 1] + grad_recv[1, layer, part].astype(F32)
            second = acc[layer, part, 2] + grad_recv[0, layer, part].astype(F32)
            inter[pl.ds(part, rows, stride=4), :] = first
            inter[pl.ds(2 + part, rows, stride=4), :] = second
        out_ref[layer * rows * 4 : (layer + 1) * rows * 4, :] = inter[...].astype(BF16)

    @pl.when(g > 0)
    def _():
        def some(s, carry):
            for j in range(side // PIECE):
                piece_copy(s, j).wait_send()
            return carry

        lax.fori_loop(0, slots, some, 0)

    @pl.when(g < last)
    def _():
        for s in range(slots):
            exit_copy(s).wait_send()

    for layer in range(2):
        for half in range(2):
            rim_copy(half, layer).wait_send()
            grad_copy(half, layer).wait_send()


def on_device(exit_grad, stored_waves, object_slices, propagator_taps, positions, counts):
    groups = lax.axis_size("depth")
    tiles = lax.axis_size("tile")
    layers, slots, side = stored_waves.shape[:3]
    own_rows = exit_grad.shape[1]
    rows = object_slices.shape[1]
    lines = layers * rows * 4
    flat_exit = exit_grad.reshape(slots, own_rows, 2, 2, 128).swapaxes(2, 3).reshape(slots * own_rows * 4, 128)
    flat_stored = (
        stored_waves.reshape(layers, slots, side, 2, 2, 128).swapaxes(3, 4).reshape(layers * slots * side * 4, 128)
    )
    flat_object = object_slices.reshape(layers, rows, 2, 2, 128).swapaxes(2, 3).reshape(lines, 128)
    vmem = pl.BlockSpec(memory_space=pltpu.VMEM)
    smem = pl.BlockSpec(memory_space=pltpu.SMEM)
    dma = pltpu.SemaphoreType.DMA
    out = pl.pallas_call(
        functools.partial(kernel, groups, tiles),
        out_shape=jax.ShapeDtypeStruct((lines, 128), BF16),
        in_specs=[smem, smem, smem, vmem, vmem, pl.BlockSpec(memory_space=pl.ANY)],
        out_specs=vmem,
        scratch_shapes=[
            pltpu.VMEM((slots, side, 2 * side), BF16),
            pltpu.VMEM((slots, side, 2 * side), BF16),
            pltpu.VMEM((slots, own_rows, 2 * side), BF16),
            pltpu.VMEM((layers, 2, 4, rows, 128), F32),
            pltpu.VMEM((layers, slots, 2, side, side), F32),
            pltpu.VMEM((layers, 2, side, side), F32),
            pltpu.VMEM((layers, 2, 4, rows, 128), F32),
            pltpu.VMEM((2, 4, 2 * rows - side, 128), F32),
            pltpu.VMEM((side * 4, 128), F32),
            pltpu.VMEM((rows * 4, 128), F32),
            pltpu.VMEM((layers * slots * side * 4, 128), BF16),
            pltpu.VMEM((2 * side, 2 * side), BF16),
            pltpu.VMEM((2, TALL, 2 * BAND), BF16),
            pltpu.VMEM((layers, 2, 336, side), BF16),
            pltpu.VMEM((2, layers, 2, rows, 128), BF16),
            pltpu.VMEM((2, layers, 2, rows, 128), BF16),
            pltpu.VMEM((2, layers, 2, rows, 128), BF16),
            pltpu.VMEM((2, layers, 2, rows, 128), BF16),
            dma((slots, 8)),
            dma((slots, 8)),
            dma((slots,)),
            dma((2, layers)),
            dma((2, layers)),
            dma((2, layers)),
            dma((2, layers)),
            dma,
        ],
        compiler_params=pltpu.CompilerParams(
            collective_id=0, has_side_effects=True, vmem_limit_bytes=48 * 1024 * 1024
        ),
    )(positions.T, counts, propagator_taps.reshape(4, propagator_taps.shape[2]), flat_exit, flat_object, flat_stored)
    return out.reshape(layers, rows, 2, 2, 128).swapaxes(2, 3).reshape(object_slices.shape)


def solution(mesh):
    return jax.shard_map(
        on_device,
        mesh=mesh,
        in_specs=(
            P("tile", "depth", None, None),
            P("depth", "tile", None, None, None),
            P("depth", None, None, "tile"),
            P(),
            P(),
            P(),
        ),
        out_specs=P("depth", None, None, "tile"),
        check_vma=False,
    )
```

```python
import functools

import jax
import jax.numpy as jnp
from jax import lax
from jax.experimental import pallas as pl
from jax.experimental.pallas import tpu as pltpu
from jax.sharding import PartitionSpec as P

MESH = pl.DeviceIdType.MESH
F32 = jnp.float32
BF16 = jnp.bfloat16

NEED = (96, 160, 224, 256)
FIRST = (80, 144, 208, 256)
SECOND = (64, 128, 192, 256)
PIECE = 32
EDGE = (0, 64, 128, 192, 256)
SHARE = 32
PAD = 16
BAND = 128
TALL = 80


def kernel(
    groups,
    tiles,
    pos_hbm,
    cnt_hbm,
    taps_hbm,
    exit_hbm,
    obj_hbm,
    st_hbm,
    out_ref,
    pos_ref,
    cnt_ref,
    taps_ref,
    exit_ref,
    obj_ref,
    waves,
    sends,
    exits,
    ext,
    win,
    back,
    acc,
    place,
    flat,
    inter,
    stored,
    mixer,
    tall,
    mixed,
    rim_send,
    rim_recv,
    grad_send,
    grad_recv,
    edge_send,
    edge_recv,
    edge,
    recv_sem,
    send_sem,
    exit_sem,
    rim_send_sem,
    rim_recv_sem,
    grad_send_sem,
    grad_recv_sem,
    exit_recv_sem,
    edge_send_sem,
    edge_recv_sem,
    load_sem,
):
    g = lax.axis_index("depth")
    t = lax.axis_index("tile")
    last = groups - 1
    side = mixer.shape[0] // 2
    slots = waves.shape[0]
    rows = ext.shape[3]
    right = lax.rem(t + 1, tiles)
    left = lax.rem(t + tiles - 1, tiles)

    barrier = pltpu.get_barrier_semaphore()

    def greet(group, tile):
        pl.semaphore_signal(barrier, inc=1, device_id=(group, tile), device_id_type=MESH)

    greet(g, right)
    greet(g, left)

    @pl.when(g == last)
    def _():
        for other in range(last):
            greet(other, t)

    @pl.when(g < last)
    def _():
        greet(last, t)

    @pl.when(g < last - 1)
    def _():
        greet(g + 1, t)

    @pl.when((g > 0) & (g < last))
    def _():
        greet(g - 1, t)

    late, early = pl.ds(0, rows * 4), pl.ds(rows * 4, rows * 4)
    sources = (exit_hbm, obj_hbm.at[early, :], obj_hbm.at[late, :], taps_hbm, pos_hbm, cnt_hbm, st_hbm)
    targets = (exit_ref, obj_ref.at[early, :], obj_ref.at[late, :], taps_ref, pos_ref, cnt_ref, stored)
    loads = [pltpu.make_async_copy(a, b, load_sem.at[k]) for k, (a, b) in enumerate(zip(sources, targets))]
    for load in loads:
        load.start()

    loads[0].wait()
    own_rows = exits.shape[1]
    lines = slots * own_rows * 4
    inter[:lines, :] = exit_ref[...].astype(F32)
    for s in range(slots):
        for part in range(2):
            for half in range(2):
                lane = part * side + half * 128
                exits[s, :, lane : lane + 128] = inter[
                    pl.ds(s * own_rows * 4 + half * 2 + part, own_rows, stride=4), :
                ].astype(BF16)

    def spread(layer):
        for part in range(2):
            for half in range(2):
                plane = obj_ref[pl.ds(layer * rows * 4 + half * 2 + part, rows, stride=4), :]
                ext[layer, part, 1 + half] = plane
                rim_send[half, layer, part] = plane.astype(BF16)

    @pl.when((g == 0) | (g == last - 1))
    def _():
        pl.semaphore_wait(barrier, 4)

    @pl.when((g > 0) & (g < last - 1))
    def _():
        pl.semaphore_wait(barrier, 5)

    @pl.when(g == last)
    def _():
        pl.semaphore_wait(barrier, last + 2)

    def exit_copy(s):
        return pltpu.make_async_remote_copy(
            src_ref=exits.at[s],
            dst_ref=waves.at[s, pl.ds(pl.multiple_of(g * SHARE, SHARE), SHARE), :],
            send_sem=exit_sem.at[s],
            recv_sem=exit_recv_sem.at[s, g],
            device_id=(last, t),
            device_id_type=MESH,
        )

    def own_exit(s):
        return pltpu.make_async_copy(
            exits.at[s],
            waves.at[s, pl.ds(last * SHARE, SHARE), :],
            exit_recv_sem.at[s, last],
        )

    def exit_arrival(s, j):
        return pltpu.make_async_copy(
            exits.at[s],
            waves.at[s, pl.ds(j * SHARE, SHARE), :],
            exit_recv_sem.at[s, j],
        )

    def exit_turn(s):
        @pl.when(g < last)
        def _():
            if s > 0:
                exit_copy(s - 1).wait_send()
            if s < slots:
                exit_copy(s).start()

    exit_turn(0)

    @pl.when(g == last)
    def _():
        for s in range(slots):
            own_exit(s).start()

    def rim_copy(half, layer):
        return pltpu.make_async_remote_copy(
            src_ref=rim_send.at[half, layer],
            dst_ref=rim_recv.at[half, layer],
            send_sem=rim_send_sem.at[half, layer],
            recv_sem=rim_recv_sem.at[half, layer],
            device_id=(g, left if half == 0 else right),
            device_id_type=MESH,
        )

    def grad_copy(half, layer):
        return pltpu.make_async_remote_copy(
            src_ref=grad_send.at[half, layer],
            dst_ref=grad_recv.at[half, layer],
            send_sem=grad_send_sem.at[half, layer],
            recv_sem=grad_recv_sem.at[half, layer],
            device_id=(g, left if half == 0 else right),
            device_id_type=MESH,
        )

    loads[1].wait()
    spread(1)
    rim_copy(0, 1).start()
    rim_copy(1, 1).start()
    exit_turn(1)
    loads[2].wait()
    spread(0)
    rim_copy(0, 0).start()
    rim_copy(1, 0).start()
    loads[3].wait()

    def mixer_rows(i, carry):
        start = pl.multiple_of(i * 32, 32)
        row = lax.broadcasted_iota(jnp.int32, (32, side), 0) + start
        column = lax.broadcasted_iota(jnp.int32, (32, side), 1)
        tap = column - row + 15
        real = jnp.zeros((32, side), F32)
        imag = jnp.zeros((32, side), F32)
        for k in range(31):
            hit = tap == k
            real = jnp.where(hit, taps_ref[2, k], real)
            imag = jnp.where(hit, taps_ref[3, k], imag)
        real = real.astype(BF16)
        imag = imag.astype(BF16)
        mixer[pl.ds(start, 32), :side] = real
        mixer[pl.ds(start, 32), side:] = -imag
        mixer[pl.ds(side + start, 32), :side] = imag
        mixer[pl.ds(side + start, 32), side:] = real
        return carry

    lax.fori_loop(0, side // 32, mixer_rows, 0)

    row = lax.broadcasted_iota(jnp.int32, (TALL, BAND), 0)
    column = lax.broadcasted_iota(jnp.int32, (TALL, BAND), 1)
    tap = row - column + 15 + PAD
    real = jnp.zeros((TALL, BAND), F32)
    imag = jnp.zeros((TALL, BAND), F32)
    for k in range(31):
        hit = tap == k
        real = jnp.where(hit, taps_ref[0, k], real)
        imag = jnp.where(hit, taps_ref[1, k], imag)
    tall[0, :, :BAND] = real.astype(BF16)
    tall[0, :, BAND:] = imag.astype(BF16)
    tall[1, :, :BAND] = -imag.astype(BF16)
    tall[1, :, BAND:] = real.astype(BF16)

    exit_turn(2)
    mixed[...] = jnp.zeros(mixed.shape, BF16)
    place[...] = jnp.zeros(place.shape, F32)
    edge[...] = jnp.zeros(edge.shape, F32)
    acc[...] = jnp.zeros(acc.shape, F32)
    for load in loads[4:]:
        load.wait()
    exit_turn(3)

    def place_of(tile, s):
        slot = tile * slots + s
        column = pos_ref[1, slot]
        block = lax.div(column, 128)
        return pos_ref[0, slot], block, column - block * 128

    def lanes(n):
        return lax.broadcasted_iota(jnp.int32, (n, 128), 1)

    def windows(s, layer, slot):
        row_start, block, turn = place_of(t, slot)
        stay = lanes(side) < 128 - turn
        for part in range(2):
            turned = [
                pltpu.roll(ext[layer, part, block + c, pl.ds(row_start, side), :], lax.rem(128 - turn, 128), 1)
                for c in range(3)
            ]
            for c in range(2):
                win[layer, s, part, :, c * 128 : c * 128 + 128] = jnp.where(stay, turned[c], turned[c + 1])

    def rim_arrived(layer):
        rim_copy(0, layer).wait_recv()
        rim_copy(1, layer).wait_recv()
        ext[layer, :, 3] = rim_recv[0, layer].astype(F32)
        ext[layer, :, 0] = rim_recv[1, layer].astype(F32)

    rim_arrived(1)
    windows(0, 1, 0)
    rim_arrived(0)
    windows(0, 0, 0)

    exit_turn(4)

    def piece_copy(s, j):
        span = pl.ds(j * PIECE, PIECE)
        return pltpu.make_async_remote_copy(
            src_ref=sends.at[s, span, :],
            dst_ref=waves.at[s, span, :],
            send_sem=send_sem.at[s, j],
            recv_sem=recv_sem.at[s, j],
            device_id=(g - 1, t),
            device_id_type=MESH,
        )

    def mix(layer, wave, begin):
        v = jnp.dot(wave, mixer[...], preferred_element_type=F32).astype(BF16)
        n = wave.shape[0]
        mixed[layer, 0, PAD + begin : PAD + begin + n, :] = v[:, :side]
        mixed[layer, 1, PAD + begin : PAD + begin + n, :] = v[:, side:]

    def leave(now, layer, begin, end):
        n = end - begin
        lhs = jnp.concatenate([tall[0, :n, :], tall[1, :n, :]], axis=0)
        rhs = jnp.concatenate(
            [mixed[layer, 0, begin : begin + BAND, :], mixed[layer, 1, begin : begin + BAND, :]], axis=0
        )
        h = jnp.dot(lhs, rhs, preferred_element_type=F32)
        real = h[:n]
        imag = h[n:]
        back[layer, 0, begin:end, :] = real
        back[layer, 1, begin:end, :] = imag
        obj_real = win[layer, now, 0, begin:end, :]
        obj_imag = win[layer, now, 1, begin:end, :]
        return jnp.concatenate(
            [obj_real * real + obj_imag * imag, obj_real * imag - obj_imag * real], axis=1
        ).astype(BF16)

    def terms(s, layer, begin, end, edges):
        n = end - begin
        live = s < cnt_ref[t]
        start = pl.multiple_of((layer * slots + s) * side * 4 + begin * 4, 64)
        flat[layer, : n * 4, :] = stored[pl.ds(start, n * 4), :].astype(F32)
        planes = [flat[layer, pl.ds(q, n, stride=4), :] for q in range(4)]
        _, block, turn = place_of(t, s)
        stay = lanes(n) >= turn
        none = jnp.zeros((n, 128), F32)
        for part in range(2):
            turned = []
            for c in range(2):
                st_real, st_imag = planes[2 * c], planes[2 * c + 1]
                real = back[layer, 0, begin:end, c * 128 : c * 128 + 128]
                imag = back[layer, 1, begin:end, c * 128 : c * 128 + 128]
                if part == 0:
                    term = st_real * real + st_imag * imag
                else:
                    term = st_real * imag - st_imag * real
                turned.append(pltpu.roll(jnp.where(live, term, 0.0), turn, 1))
            three = (
                jnp.where(stay, turned[0], none),
                jnp.where(stay, turned[1], turned[0]),
                jnp.where(stay, none, turned[1]),
            )
            for c in range(3):
                place[layer, part, c, rows - side + begin : rows - side + end, :] = three[c]
            if not edges:
                continue
            lane = (layer * 2 + part) * 128
            edge_send[0, begin:end, lane : lane + 128] = jnp.where(block == 0, three[0], none).astype(BF16)
            edge_send[1, begin:end, lane : lane + 128] = jnp.where(block == 0, none, three[2]).astype(BF16)

    def add_terms(s, layer, columns):
        row_start, block, _ = place_of(t, s)
        for part in range(2):
            for c in columns:
                acc[layer, part, c] += place[
                    layer, part, lax.rem(c + 4 - block, 4), pl.ds(rows - side - row_start, rows), :
                ]

    def edge_copy(half, step):
        span = pl.ds(EDGE[step], EDGE[step + 1] - EDGE[step])
        return pltpu.make_async_remote_copy(
            src_ref=edge_send.at[half, span, :],
            dst_ref=edge_recv.at[half, span, :],
            send_sem=edge_send_sem.at[half, step],
            recv_sem=edge_recv_sem.at[half, step],
            device_id=(g, left if half == 0 else right),
            device_id_type=MESH,
        )

    def send_grad(layer):
        grad_send[0, layer] = acc[layer, :, 0].astype(BF16)
        grad_send[1, layer] = acc[layer, :, 3].astype(BF16)
        grad_copy(0, layer).start()
        grad_copy(1, layer).start()

    def last_terms(step):
        for at in range(EDGE[step], EDGE[step + 1], 64):
            for layer in (1, 0):
                terms(slots - 1, layer, at, at + 64, True)
        edge_copy(0, step).start()
        edge_copy(1, step).start()

    def relay(s, final):
        now = lax.rem(s, 2)
        came = first_end = second_end = 0
        for step in range(len(NEED)):

            @pl.when(g < last)
            def _():
                for j in range(came // PIECE, NEED[step] // PIECE):
                    piece_copy(s, j).wait_recv()

            @pl.when(g == last)
            def _():
                for j in range(pl.cdiv(came, SHARE), pl.cdiv(NEED[step], SHARE)):
                    exit_arrival(s, j).wait()

            mix(1, waves[s, came : NEED[step], :], came)
            if step < 2 and not final:
                windows(1 - now, 1 - step, s + 1)
            wave = leave(now, 1, first_end, FIRST[step])
            mix(0, wave, first_end)
            sends[s, second_end : SECOND[step], :] = leave(now, 0, second_end, SECOND[step])

            @pl.when(g > 0)
            def _():
                for j in range(second_end // PIECE, SECOND[step] // PIECE):
                    piece_copy(s, j).start()

            if final and step == 0:
                send_grad(1)
                send_grad(0)
            if final and step < 2:
                pl.when(g == 0)(functools.partial(last_terms, step))
            came, first_end, second_end = NEED[step], FIRST[step], SECOND[step]

    def turn(s, carry):
        relay(s, False)
        for layer in (1, 0):
            for at in range(0, side, 64):
                terms(s, layer, at, at + 64, False)
            add_terms(s, layer, range(4))
        return carry

    lax.fori_loop(0, slots - 1, turn, 0)
    relay(slots - 1, True)

    @pl.when(g > 0)
    def _():
        last_terms(0)
        last_terms(1)

    last_terms(2)
    last_terms(3)
    for layer in (1, 0):
        add_terms(slots - 1, layer, (1, 2))
        for half in range(2):
            grad_copy(half, layer).wait_recv()
        for part in range(2):
            acc[layer, part, 1] += grad_recv[1, layer, part].astype(F32)
            acc[layer, part, 2] += grad_recv[0, layer, part].astype(F32)

    for step in range(len(EDGE) - 1):
        for half in range(2):
            edge_copy(half, step).wait_recv()
            begin, end = EDGE[step], EDGE[step + 1]
            for k in range(4):
                edge[half, k, rows - side + begin : rows - side + end, :] = edge_recv[
                    half, begin:end, k * 128 : k * 128 + 128
                ].astype(F32)

    left_rows = place_of(left, slots - 1)[0]
    right_rows = place_of(right, slots - 1)[0]
    for layer in (1, 0):
        for part in range(2):
            k = layer * 2 + part
            first = acc[layer, part, 1] + edge[1, k, pl.ds(rows - side - left_rows, rows), :]
            second = acc[layer, part, 2] + edge[0, k, pl.ds(rows - side - right_rows, rows), :]
            inter[pl.ds(part, rows, stride=4), :] = first
            inter[pl.ds(2 + part, rows, stride=4), :] = second
        out_ref[layer * rows * 4 : (layer + 1) * rows * 4, :] = inter[...].astype(BF16)

    @pl.when(g > 0)
    def _():
        def some(s, carry):
            for j in range(side // PIECE):
                piece_copy(s, j).wait_send()
            return carry

        lax.fori_loop(0, slots, some, 0)

    for half in range(2):
        for layer in range(2):
            rim_copy(half, layer).wait_send()
            grad_copy(half, layer).wait_send()
        for step in range(len(EDGE) - 1):
            edge_copy(half, step).wait_send()


def on_device(exit_grad, stored_waves, object_slices, propagator_taps, positions, counts):
    groups = lax.axis_size("depth")
    tiles = lax.axis_size("tile")
    layers, slots, side = stored_waves.shape[:3]
    own_rows = exit_grad.shape[1]
    rows = object_slices.shape[1]
    lines = layers * rows * 4
    flat_exit = exit_grad.reshape(slots, own_rows, 2, 2, 128).swapaxes(2, 3).reshape(slots * own_rows * 4, 128)
    flat_stored = (
        stored_waves.reshape(layers, slots, side, 2, 2, 128).swapaxes(3, 4).reshape(layers * slots * side * 4, 128)
    )
    flat_object = object_slices.reshape(layers, rows, 2, 2, 128).swapaxes(2, 3).reshape(lines, 128)
    vmem = pl.BlockSpec(memory_space=pltpu.VMEM)
    dma = pltpu.SemaphoreType.DMA
    out = pl.pallas_call(
        functools.partial(kernel, groups, tiles),
        out_shape=jax.ShapeDtypeStruct((lines, 128), BF16),
        in_specs=[pl.BlockSpec(memory_space=pltpu.HBM)] * 6,
        out_specs=vmem,
        scratch_shapes=[
            pltpu.SMEM((2, positions.shape[0]), jnp.int32),
            pltpu.SMEM(counts.shape, jnp.int32),
            pltpu.SMEM((4, propagator_taps.shape[2]), F32),
            pltpu.VMEM(flat_exit.shape, BF16),
            pltpu.VMEM(flat_object.shape, F32),
            pltpu.VMEM((slots, side, 2 * side), BF16),
            pltpu.VMEM((slots, side, 2 * side), BF16),
            pltpu.VMEM((slots, own_rows, 2 * side), BF16),
            pltpu.VMEM((layers, 2, 4, rows, 128), F32),
            pltpu.VMEM((layers, 2, 2, side, side), F32),
            pltpu.VMEM((layers, 2, side, side), F32),
            pltpu.VMEM((layers, 2, 4, rows, 128), F32),
            pltpu.VMEM((layers, 2, 4, 2 * rows - side, 128), F32),
            pltpu.VMEM((layers, side * 4, 128), F32),
            pltpu.VMEM((rows * 4, 128), F32),
            pltpu.VMEM((layers * slots * side * 4, 128), BF16),
            pltpu.VMEM((2 * side, 2 * side), BF16),
            pltpu.VMEM((2, TALL, 2 * BAND), BF16),
            pltpu.VMEM((layers, 2, 336, side), BF16),
            pltpu.VMEM((2, layers, 2, rows, 128), BF16),
            pltpu.VMEM((2, layers, 2, rows, 128), BF16),
            pltpu.VMEM((2, layers, 2, rows, 128), BF16),
            pltpu.VMEM((2, layers, 2, rows, 128), BF16),
            pltpu.VMEM((2, side, 2 * layers * 128), BF16),
            pltpu.VMEM((2, side, 2 * layers * 128), BF16),
            pltpu.VMEM((2, 2 * layers, 2 * rows - side, 128), F32),
            dma((slots, side // PIECE)),
            dma((slots, side // PIECE)),
            dma((slots,)),
            dma((2, layers)),
            dma((2, layers)),
            dma((2, layers)),
            dma((2, layers)),
            dma((slots, groups)),
            dma((2, len(EDGE) - 1)),
            dma((2, len(EDGE) - 1)),
            dma((7,)),
        ],
        compiler_params=pltpu.CompilerParams(
            collective_id=0, has_side_effects=True, vmem_limit_bytes=48 * 1024 * 1024
        ),
    )(
        *(
            pltpu.with_memory_space_constraint(x, pltpu.HBM)
            for x in (
                positions.T,
                counts,
                propagator_taps.reshape(4, propagator_taps.shape[2]),
                flat_exit,
                flat_object,
                flat_stored,
            )
        )
    )
    return out.reshape(layers, rows, 2, 2, 128).swapaxes(2, 3).reshape(object_slices.shape)


def solution(mesh):
    return jax.shard_map(
        on_device,
        mesh=mesh,
        in_specs=(
            P("tile", "depth", None, None),
            P("depth", "tile", None, None, None),
            P("depth", None, None, "tile"),
            P(),
            P(),
            P(),
        ),
        out_specs=P("depth", None, None, "tile"),
        check_vma=False,
    )
```

```python
import functools

import jax
import jax.numpy as jnp
from jax import lax
from jax.experimental import pallas as pl
from jax.experimental.pallas import tpu as pltpu
from jax.sharding import PartitionSpec as P

MESH = pl.DeviceIdType.MESH
F32 = jnp.float32
BF16 = jnp.bfloat16

NEED = (96, 128, 160, 192, 224, 256)
FIRST = (80, 112, 144, 176, 208, 256)
SECOND = (64, 96, 128, 160, 192, 256)
PIECE = 32
EDGE = (0, 64, 128, 192, 256)
SHARE = 32
PAD = 16
BAND = 128
TALL = 80


def kernel(
    groups,
    tiles,
    pos_hbm,
    cnt_hbm,
    taps_hbm,
    exit_hbm,
    obj_hbm,
    st_hbm,
    out_ref,
    pos_ref,
    cnt_ref,
    taps_ref,
    exit_ref,
    obj_ref,
    waves,
    sends,
    exits,
    ext,
    win,
    back,
    acc,
    place,
    flat,
    inter,
    stored,
    mixer,
    tall,
    mixed,
    rim_send,
    rim_recv,
    grad_send,
    grad_recv,
    edge_send,
    edge_recv,
    edge,
    recv_sem,
    send_sem,
    exit_sem,
    rim_send_sem,
    rim_recv_sem,
    grad_send_sem,
    grad_recv_sem,
    exit_recv_sem,
    edge_send_sem,
    edge_recv_sem,
    load_sem,
):
    g = lax.axis_index("depth")
    t = lax.axis_index("tile")
    last = groups - 1
    side = mixer.shape[0] // 2
    slots = waves.shape[0]
    rows = ext.shape[3]
    right = lax.rem(t + 1, tiles)
    left = lax.rem(t + tiles - 1, tiles)

    barrier = pltpu.get_barrier_semaphore()

    def greet(group, tile):
        pl.semaphore_signal(barrier, inc=1, device_id=(group, tile), device_id_type=MESH)

    greet(g, right)
    greet(g, left)

    @pl.when(g == last)
    def _():
        for other in range(last):
            greet(other, t)

    @pl.when(g < last)
    def _():
        greet(last, t)

    @pl.when(g < last - 1)
    def _():
        greet(g + 1, t)

    @pl.when((g > 0) & (g < last))
    def _():
        greet(g - 1, t)

    late, early = pl.ds(0, rows * 4), pl.ds(rows * 4, rows * 4)
    sources = (exit_hbm, obj_hbm.at[early, :], obj_hbm.at[late, :], taps_hbm, pos_hbm, cnt_hbm, st_hbm)
    targets = (exit_ref, obj_ref.at[early, :], obj_ref.at[late, :], taps_ref, pos_ref, cnt_ref, stored)
    loads = [pltpu.make_async_copy(a, b, load_sem.at[k]) for k, (a, b) in enumerate(zip(sources, targets))]
    for load in loads:
        load.start()

    loads[0].wait()
    own_rows = exits.shape[1]
    lines = slots * own_rows * 4
    inter[:lines, :] = exit_ref[...].astype(F32)
    for s in range(slots):
        for part in range(2):
            for half in range(2):
                lane = part * side + half * 128
                exits[s, :, lane : lane + 128] = inter[
                    pl.ds(s * own_rows * 4 + half * 2 + part, own_rows, stride=4), :
                ].astype(BF16)

    def spread(layer):
        for part in range(2):
            for half in range(2):
                plane = obj_ref[pl.ds(layer * rows * 4 + half * 2 + part, rows, stride=4), :]
                ext[layer, part, 1 + half] = plane
                rim_send[half, layer, part] = plane.astype(BF16)

    @pl.when((g == 0) | (g == last - 1))
    def _():
        pl.semaphore_wait(barrier, 4)

    @pl.when((g > 0) & (g < last - 1))
    def _():
        pl.semaphore_wait(barrier, 5)

    @pl.when(g == last)
    def _():
        pl.semaphore_wait(barrier, last + 2)

    def exit_copy(s):
        return pltpu.make_async_remote_copy(
            src_ref=exits.at[s],
            dst_ref=waves.at[s, pl.ds(pl.multiple_of(g * SHARE, SHARE), SHARE), :],
            send_sem=exit_sem.at[s],
            recv_sem=exit_recv_sem.at[s, g],
            device_id=(last, t),
            device_id_type=MESH,
        )

    def own_exit(s):
        return pltpu.make_async_copy(
            exits.at[s],
            waves.at[s, pl.ds(last * SHARE, SHARE), :],
            exit_recv_sem.at[s, last],
        )

    def exit_arrival(s, j):
        return pltpu.make_async_copy(
            exits.at[s],
            waves.at[s, pl.ds(j * SHARE, SHARE), :],
            exit_recv_sem.at[s, j],
        )

    def exit_turn(s):
        @pl.when(g < last)
        def _():
            if s > 0:
                exit_copy(s - 1).wait_send()
            if s < slots:
                exit_copy(s).start()

    exit_turn(0)

    @pl.when(g == last)
    def _():
        for s in range(slots):
            own_exit(s).start()

    def rim_copy(half, layer):
        return pltpu.make_async_remote_copy(
            src_ref=rim_send.at[half, layer],
            dst_ref=rim_recv.at[half, layer],
            send_sem=rim_send_sem.at[half, layer],
            recv_sem=rim_recv_sem.at[half, layer],
            device_id=(g, left if half == 0 else right),
            device_id_type=MESH,
        )

    def grad_copy(half, layer):
        return pltpu.make_async_remote_copy(
            src_ref=grad_send.at[half, layer],
            dst_ref=grad_recv.at[half, layer],
            send_sem=grad_send_sem.at[half, layer],
            recv_sem=grad_recv_sem.at[half, layer],
            device_id=(g, left if half == 0 else right),
            device_id_type=MESH,
        )

    loads[1].wait()
    spread(1)
    rim_copy(0, 1).start()
    rim_copy(1, 1).start()
    exit_turn(1)
    loads[2].wait()
    spread(0)
    rim_copy(0, 0).start()
    rim_copy(1, 0).start()
    loads[3].wait()

    def mixer_rows(i, carry):
        start = pl.multiple_of(i * 32, 32)
        row = lax.broadcasted_iota(jnp.int32, (32, side), 0) + start
        column = lax.broadcasted_iota(jnp.int32, (32, side), 1)
        tap = column - row + 15
        real = jnp.zeros((32, side), F32)
        imag = jnp.zeros((32, side), F32)
        for k in range(31):
            hit = tap == k
            real = jnp.where(hit, taps_ref[2, k], real)
            imag = jnp.where(hit, taps_ref[3, k], imag)
        real = real.astype(BF16)
        imag = imag.astype(BF16)
        mixer[pl.ds(start, 32), :side] = real
        mixer[pl.ds(start, 32), side:] = -imag
        mixer[pl.ds(side + start, 32), :side] = imag
        mixer[pl.ds(side + start, 32), side:] = real
        return carry

    lax.fori_loop(0, side // 32, mixer_rows, 0)

    row = lax.broadcasted_iota(jnp.int32, (TALL, BAND), 0)
    column = lax.broadcasted_iota(jnp.int32, (TALL, BAND), 1)
    tap = row - column + 15 + PAD
    real = jnp.zeros((TALL, BAND), F32)
    imag = jnp.zeros((TALL, BAND), F32)
    for k in range(31):
        hit = tap == k
        real = jnp.where(hit, taps_ref[0, k], real)
        imag = jnp.where(hit, taps_ref[1, k], imag)
    tall[0, :, :BAND] = real.astype(BF16)
    tall[0, :, BAND:] = imag.astype(BF16)
    tall[1, :, :BAND] = -imag.astype(BF16)
    tall[1, :, BAND:] = real.astype(BF16)

    exit_turn(2)
    place[...] = jnp.zeros(place.shape, F32)
    edge[...] = jnp.zeros(edge.shape, F32)
    acc[...] = jnp.zeros(acc.shape, F32)
    for load in loads[4:]:
        load.wait()
    exit_turn(3)

    def place_of(tile, s):
        slot = tile * slots + s
        column = pos_ref[1, slot]
        block = lax.div(column, 128)
        return pos_ref[0, slot], block, column - block * 128

    def lanes(n):
        return lax.broadcasted_iota(jnp.int32, (n, 128), 1)

    def windows(s, layer, slot):
        row_start, block, turn = place_of(t, slot)
        stay = lanes(side) < 128 - turn
        for part in range(2):
            turned = [
                pltpu.roll(ext[layer, part, block + c, pl.ds(row_start, side), :], lax.rem(128 - turn, 128), 1)
                for c in range(3)
            ]
            for c in range(2):
                win[layer, s, part, :, c * 128 : c * 128 + 128] = jnp.where(stay, turned[c], turned[c + 1])

    def rim_arrived(layer):
        rim_copy(0, layer).wait_recv()
        rim_copy(1, layer).wait_recv()
        ext[layer, :, 3] = rim_recv[0, layer].astype(F32)
        ext[layer, :, 0] = rim_recv[1, layer].astype(F32)

    rim_arrived(1)
    windows(0, 1, 0)
    rim_arrived(0)
    windows(0, 0, 0)

    exit_turn(4)

    def piece_copy(s, j):
        span = pl.ds(j * PIECE, PIECE)
        return pltpu.make_async_remote_copy(
            src_ref=sends.at[s, span, :],
            dst_ref=waves.at[s, span, :],
            send_sem=send_sem.at[s, j],
            recv_sem=recv_sem.at[s, j],
            device_id=(g - 1, t),
            device_id_type=MESH,
        )

    def mix(layer, wave, begin):
        v = jnp.dot(wave, mixer[...], preferred_element_type=F32).astype(BF16)
        n = wave.shape[0]
        blocks = []
        for part in range(2):
            half = v[:, part * side : (part + 1) * side]
            above = mixed[layer, part] if begin else jnp.zeros((PAD, side), BF16)
            rest = jnp.zeros((BAND - n - above.shape[0], side), BF16)
            blocks += [above, half, rest]
            mixed[layer, part] = half[n - 2 * PAD :]
        return jnp.concatenate(blocks, axis=0)

    def leave(s, now, layer, begin, end, rhs):
        n = end - begin
        lhs = jnp.concatenate([tall[0, :n, :], tall[1, :n, :]], axis=0)
        h = jnp.dot(lhs, rhs, preferred_element_type=F32)
        real = h[:n]
        imag = h[n:]
        back[s, layer, 0, begin:end, :] = real
        back[s, layer, 1, begin:end, :] = imag
        obj_real = win[layer, now, 0, begin:end, :]
        obj_imag = win[layer, now, 1, begin:end, :]
        return jnp.concatenate(
            [obj_real * real + obj_imag * imag, obj_real * imag - obj_imag * real], axis=1
        ).astype(BF16)

    def terms(s, layer, begin, end, edges):
        n = end - begin
        live = s < cnt_ref[t]
        start = pl.multiple_of((layer * slots + s) * side * 4 + begin * 4, 64)
        flat[layer, : n * 4, :] = stored[pl.ds(start, n * 4), :].astype(F32)
        planes = [flat[layer, pl.ds(q, n, stride=4), :] for q in range(4)]
        _, block, turn = place_of(t, s)
        stay = lanes(n) >= turn
        none = jnp.zeros((n, 128), F32)
        for part in range(2):
            turned = []
            for c in range(2):
                st_real, st_imag = planes[2 * c], planes[2 * c + 1]
                real = back[s, layer, 0, begin:end, c * 128 : c * 128 + 128]
                imag = back[s, layer, 1, begin:end, c * 128 : c * 128 + 128]
                if part == 0:
                    term = st_real * real + st_imag * imag
                else:
                    term = st_real * imag - st_imag * real
                turned.append(pltpu.roll(jnp.where(live, term, 0.0), turn, 1))
            three = (
                jnp.where(stay, turned[0], none),
                jnp.where(stay, turned[1], turned[0]),
                jnp.where(stay, none, turned[1]),
            )
            for c in range(3):
                place[layer, part, c, rows - side + begin : rows - side + end, :] = three[c]
            if not edges:
                continue
            lane = (layer * 2 + part) * 128
            edge_send[0, begin:end, lane : lane + 128] = jnp.where(block == 0, three[0], none).astype(BF16)
            edge_send[1, begin:end, lane : lane + 128] = jnp.where(block == 0, none, three[2]).astype(BF16)

    def add_terms(s, layer, columns):
        row_start, block, _ = place_of(t, s)
        for part in range(2):
            for c in columns:
                acc[layer, part, c] += place[
                    layer, part, lax.rem(c + 4 - block, 4), pl.ds(rows - side - row_start, rows), :
                ]

    def edge_copy(half, step):
        span = pl.ds(EDGE[step], EDGE[step + 1] - EDGE[step])
        return pltpu.make_async_remote_copy(
            src_ref=edge_send.at[half, span, :],
            dst_ref=edge_recv.at[half, span, :],
            send_sem=edge_send_sem.at[half, step],
            recv_sem=edge_recv_sem.at[half, step],
            device_id=(g, left if half == 0 else right),
            device_id_type=MESH,
        )

    def send_grad(layer):
        grad_send[0, layer] = acc[layer, :, 0].astype(BF16)
        grad_send[1, layer] = acc[layer, :, 3].astype(BF16)
        grad_copy(0, layer).start()
        grad_copy(1, layer).start()

    def last_terms(step):
        for at in range(EDGE[step], EDGE[step + 1], 64):
            for layer in (1, 0):
                terms(slots - 1, layer, at, at + 64, True)
        edge_copy(0, step).start()
        edge_copy(1, step).start()

    def send_grads():
        send_grad(1)
        send_grad(0)

    def collect(s, carry):
        for layer in (1, 0):
            for at in range(0, side, 64):
                terms(s, layer, at, at + 64, False)
            add_terms(s, layer, range(4))
        return carry

    def relay(s, final):
        now = lax.rem(s, 2)
        came = first_end = second_end = 0
        for step in range(len(NEED)):

            @pl.when(g < last)
            def _():
                for j in range(came // PIECE, NEED[step] // PIECE):
                    piece_copy(s, j).wait_recv()

            @pl.when(g == last)
            def _():
                for j in range(pl.cdiv(came, SHARE), pl.cdiv(NEED[step], SHARE)):
                    exit_arrival(s, j).wait()

            rhs = mix(1, waves[s, came : NEED[step], :], came)
            if step < 2 and not final:
                windows(1 - now, 1 - step, s + 1)
            wave = leave(s, now, 1, first_end, FIRST[step], rhs)
            rhs = mix(0, wave, first_end)
            sends[s, second_end : SECOND[step], :] = leave(s, now, 0, second_end, SECOND[step], rhs)

            @pl.when(g > 0)
            def _():
                for j in range(second_end // PIECE, SECOND[step] // PIECE):
                    piece_copy(s, j).start()

            if final and step == 0:
                pl.when(g <= 1)(send_grads)
            if final and step in (0, 2):
                pl.when(g == 0)(functools.partial(last_terms, step // 2))
            came, first_end, second_end = NEED[step], FIRST[step], SECOND[step]

    def turn(s, carry):
        relay(s, False)

        @pl.when(g <= 1)
        def _():
            collect(s, 0)

        return carry

    lax.fori_loop(0, slots - 1, turn, 0)
    relay(slots - 1, True)

    @pl.when(g > 1)
    def _():
        lax.fori_loop(0, slots - 1, collect, 0)
        send_grads()

    @pl.when(g > 0)
    def _():
        last_terms(0)
        last_terms(1)

    last_terms(2)
    last_terms(3)
    for layer in (1, 0):
        add_terms(slots - 1, layer, (1, 2))
        for half in range(2):
            grad_copy(half, layer).wait_recv()
        for part in range(2):
            acc[layer, part, 1] += grad_recv[1, layer, part].astype(F32)
            acc[layer, part, 2] += grad_recv[0, layer, part].astype(F32)

    for step in range(len(EDGE) - 1):
        for half in range(2):
            edge_copy(half, step).wait_recv()
            begin, end = EDGE[step], EDGE[step + 1]
            for k in range(4):
                edge[half, k, rows - side + begin : rows - side + end, :] = edge_recv[
                    half, begin:end, k * 128 : k * 128 + 128
                ].astype(F32)

    left_rows = place_of(left, slots - 1)[0]
    right_rows = place_of(right, slots - 1)[0]
    for layer in (1, 0):
        for part in range(2):
            k = layer * 2 + part
            first = acc[layer, part, 1] + edge[1, k, pl.ds(rows - side - left_rows, rows), :]
            second = acc[layer, part, 2] + edge[0, k, pl.ds(rows - side - right_rows, rows), :]
            inter[pl.ds(part, rows, stride=4), :] = first
            inter[pl.ds(2 + part, rows, stride=4), :] = second
        out_ref[layer * rows * 4 : (layer + 1) * rows * 4, :] = inter[...].astype(BF16)

    @pl.when(g > 0)
    def _():
        def some(s, carry):
            for j in range(side // PIECE):
                piece_copy(s, j).wait_send()
            return carry

        lax.fori_loop(0, slots, some, 0)

    for half in range(2):
        for layer in range(2):
            rim_copy(half, layer).wait_send()
            grad_copy(half, layer).wait_send()
        for step in range(len(EDGE) - 1):
            edge_copy(half, step).wait_send()


def on_device(exit_grad, stored_waves, object_slices, propagator_taps, positions, counts):
    groups = lax.axis_size("depth")
    tiles = lax.axis_size("tile")
    layers, slots, side = stored_waves.shape[:3]
    own_rows = exit_grad.shape[1]
    rows = object_slices.shape[1]
    lines = layers * rows * 4
    flat_exit = exit_grad.reshape(slots, own_rows, 2, 2, 128).swapaxes(2, 3).reshape(slots * own_rows * 4, 128)
    flat_stored = (
        stored_waves.reshape(layers, slots, side, 2, 2, 128).swapaxes(3, 4).reshape(layers * slots * side * 4, 128)
    )
    flat_object = object_slices.reshape(layers, rows, 2, 2, 128).swapaxes(2, 3).reshape(lines, 128)
    vmem = pl.BlockSpec(memory_space=pltpu.VMEM)
    dma = pltpu.SemaphoreType.DMA
    out = pl.pallas_call(
        functools.partial(kernel, groups, tiles),
        out_shape=jax.ShapeDtypeStruct((lines, 128), BF16),
        in_specs=[pl.BlockSpec(memory_space=pltpu.HBM)] * 6,
        out_specs=vmem,
        scratch_shapes=[
            pltpu.SMEM((2, positions.shape[0]), jnp.int32),
            pltpu.SMEM(counts.shape, jnp.int32),
            pltpu.SMEM((4, propagator_taps.shape[2]), F32),
            pltpu.VMEM(flat_exit.shape, BF16),
            pltpu.VMEM(flat_object.shape, F32),
            pltpu.VMEM((slots, side, 2 * side), BF16),
            pltpu.VMEM((slots, side, 2 * side), BF16),
            pltpu.VMEM((slots, own_rows, 2 * side), BF16),
            pltpu.VMEM((layers, 2, 4, rows, 128), F32),
            pltpu.VMEM((layers, 2, 2, side, side), F32),
            pltpu.VMEM((slots, layers, 2, side, side), F32),
            pltpu.VMEM((layers, 2, 4, rows, 128), F32),
            pltpu.VMEM((layers, 2, 4, 2 * rows - side, 128), F32),
            pltpu.VMEM((layers, side * 4, 128), F32),
            pltpu.VMEM((rows * 4, 128), F32),
            pltpu.VMEM((layers * slots * side * 4, 128), BF16),
            pltpu.VMEM((2 * side, 2 * side), BF16),
            pltpu.VMEM((2, TALL, 2 * BAND), BF16),
            pltpu.VMEM((layers, 2, 2 * PAD, side), BF16),
            pltpu.VMEM((2, layers, 2, rows, 128), BF16),
            pltpu.VMEM((2, layers, 2, rows, 128), BF16),
            pltpu.VMEM((2, layers, 2, rows, 128), BF16),
            pltpu.VMEM((2, layers, 2, rows, 128), BF16),
            pltpu.VMEM((2, side, 2 * layers * 128), BF16),
            pltpu.VMEM((2, side, 2 * layers * 128), BF16),
            pltpu.VMEM((2, 2 * layers, 2 * rows - side, 128), F32),
            dma((slots, side // PIECE)),
            dma((slots, side // PIECE)),
            dma((slots,)),
            dma((2, layers)),
            dma((2, layers)),
            dma((2, layers)),
            dma((2, layers)),
            dma((slots, groups)),
            dma((2, len(EDGE) - 1)),
            dma((2, len(EDGE) - 1)),
            dma((7,)),
        ],
        compiler_params=pltpu.CompilerParams(
            collective_id=0, has_side_effects=True, vmem_limit_bytes=48 * 1024 * 1024
        ),
    )(
        *(
            pltpu.with_memory_space_constraint(x, pltpu.HBM)
            for x in (
                positions.T,
                counts,
                propagator_taps.reshape(4, propagator_taps.shape[2]),
                flat_exit,
                flat_object,
                flat_stored,
            )
        )
    )
    return out.reshape(layers, rows, 2, 2, 128).swapaxes(2, 3).reshape(object_slices.shape)


def solution(mesh):
    return jax.shard_map(
        on_device,
        mesh=mesh,
        in_specs=(
            P("tile", "depth", None, None),
            P("depth", "tile", None, None, None),
            P("depth", None, None, "tile"),
            P(),
            P(),
            P(),
        ),
        out_specs=P("depth", None, None, "tile"),
        check_vma=False,
    )
```
